32 devices in a mesh: tile: 8 (over z, core), dp: 4 (over y, x).
Axes of the slice: x: 2, y: 2, z: 4, core: 2. Of those that a mesh axis runs over, the one named last changes fastest.
Arguments:
- clip_frames: bfloat16 [4, 8, 32, 8, 128], P('dp', None, 'tile'), may hold values from -6 to 6
- segments: int32 [4, 8], P('dp'), may hold values from 0 to 2, never falling along the last dimension, each value on 1 to 4 neighbouring positions
- weight_first: bfloat16 [3456, 128], replicated, may hold values from -0.109375 to 0.109375
- weight_second: bfloat16 [3456, 128], replicated, may hold values from -0.109375 to 0.109375
- cotangent: bfloat16 [4, 8, 16, 4, 128], P('dp', None, 'tile'), may hold values from -6 to 6
Outputs:
- pooled: float32 [4, 8, 16, 4, 128], P('dp', None, 'tile')
- input_grad: float32 [4, 8, 32, 8, 128], P('dp', None, 'tile')
- grad_first: float32 [3456, 128], P('tile')
- grad_second: float32 [3456, 128], P('tile')
The draws below stay inside these ranges and needn't reach their ends.
Inputs may be any that keep to these rules, and one draw needn't show every extreme that they name: `segments`: clip numbers never fall along the frames of a sequence; each clip is one to 4 frames long and one clip has exactly 4.
All inputs are finite; a program needn't handle non-finite values.
Results may differ from the reference program's by a relative error of at most 0.0029.
Values may be sent and summed in bfloat16 or wider, within the bound.
A program may use at most 64 MiB of HBM per device.

```python
import math
import jax
import jax.numpy as jnp
import numpy as np
from jax import lax

C = 128
FRAMES = 8
WW = 8
GROUPS = 4
H = 32


def block_scale(stream_key, extent, cuts, low, top_value):
    level = 1.0
    for dim, shards_of in cuts:
        heights = jax.random.uniform(jax.random.fold_in(jax.random.fold_in(stream_key, 6), dim), (shards_of,), jnp.float32, low / len(cuts), top_value / len(cuts))
        level = level * jnp.repeat(jnp.exp(heights), extent[dim] // shards_of).reshape((-1,) + (1,) * (len(extent) - 1 - dim))
    return level


def profile(amount, total, bound, skew):
    loads = [(1 << 20) // math.isqrt(grade ** skew) + 1 for grade in range(2, amount + 1)]
    rest, given = total - bound - (amount - 1), [1] * (amount - 1)
    while rest > 0:
        free = [i for i in range(amount - 1) if given[i] < bound]
        whole, budget = sum([loads[i] for i in free]), rest
        for i in free:
            more = min(bound - given[i], max(1, budget * loads[i] // whole), rest)
            given[i] = given[i] + more
            rest = rest - more
    return np.array([bound] + given)


def ragged(stream_key, number_of, total, most, skew):
    if number_of == 2:
        one = jax.random.randint(stream_key, (), max(1, total - most), min(most, total - 1) + 1)
        return jnp.stack([one, total - one])
    tallies = jnp.asarray(profile(number_of, total, most, skew), jnp.int32)
    pairs = (number_of - 1) // 2
    giver, taker = tallies[1:1 + 2 * pairs:2], tallies[2:2 + 2 * pairs:2]
    margin = jnp.minimum(giver - 1, most - taker)
    moved = jax.random.randint(jax.random.fold_in(stream_key, 1), (pairs,), 0, 1 << 20) % (margin + 1)
    tallies = tallies.at[1:1 + 2 * pairs:2].set(giver - moved).at[2:2 + 2 * pairs:2].set(taker + moved)
    return tallies[jax.random.permutation(jax.random.fold_in(stream_key, 2), number_of)]


def centred(stream_key, extent, spread, limit, cuts=(), held_as=jnp.bfloat16):
    values = jax.random.normal(stream_key, extent, jnp.float32) * spread
    if len(cuts) > 0:
        values = block_scale(stream_key, extent, cuts, -0.22, 0.18) * values
    return jnp.clip(values, min=-limit, max=limit).astype(held_as)


def setup_inputs(seed: int = 0) -> dict:
    streams_of = jax.random.split(jax.random.key(seed), 6)
    return {
        "clip_frames": centred(streams_of[0], (GROUPS, FRAMES, H, WW, C), 1.0, 6.0, ((0, 4), (2, 8))),
        "segments": jax.vmap(lambda own: jnp.searchsorted(jnp.cumsum(ragged(own, FRAMES // 4 + 1, FRAMES, FRAMES // 2, 1)), jnp.arange(FRAMES), side="right"))(jax.random.split(streams_of[1], GROUPS)).reshape((GROUPS, FRAMES)).astype(jnp.int32),
        "weight_first": centred(streams_of[2], (27 * C, C), (27 * C) ** -0.5, 0.109375),
        "weight_second": centred(streams_of[3], (27 * C, C), (27 * C) ** -0.5, 0.109375),
        "cotangent": centred(streams_of[4], (GROUPS, FRAMES, H // 2, WW // 2, C), 1.0, 6.0, ((0, 4), (2, 8))),
    }


def make_masks(clip_ids):
    frame_count = clip_ids.shape[0]
    result = []
    for delay_step in range(3):
        earlier = jnp.concatenate([jnp.full((delay_step,), -1, jnp.int32), clip_ids[:frame_count - delay_step].astype(jnp.int32)])
        result.append(earlier == clip_ids.astype(jnp.int32))
    return result

def move_frames(field, delay_step, reverse):
    if delay_step == 0:
        return field
    filler = jnp.zeros((delay_step,) + field.shape[1:], field.dtype)
    if reverse:
        return jnp.concatenate([field[delay_step:], filler], axis=0)
    return jnp.concatenate([filler, field[:field.shape[0] - delay_step]], axis=0)

def tap_columns(padded, frame_masks, reverse, row_count, col_count):
    channels = padded.shape[-1]
    pieces = []
    for delay_step in range(3):
        keep = frame_masks[delay_step]
        if reverse:
            keep = move_frames(keep, delay_step, True)
        moved = jnp.where(keep[:, None, None, None], move_frames(padded, delay_step, reverse), jnp.zeros((), padded.dtype))
        for row_tap in range(3):
            for col_tap in range(3):
                row_at = 2 - row_tap if reverse else row_tap
                col_at = 2 - col_tap if reverse else col_tap
                pieces.append(moved[:, row_at:row_at + row_count, col_at:col_at + col_count, :])
    return jnp.concatenate(pieces, axis=-1).reshape(-1, 27 * channels)

def flip_kernel(kernel):
    channels = kernel.shape[1]
    return kernel.reshape(27, channels, channels).transpose(0, 2, 1).reshape(27 * channels, channels)

def pad_both(field):
    return jnp.pad(field, ((0, 0), (1, 1), (1, 1), (0, 0)))

def one_group(frames_one, clip_ids, cot_one, weight_first, weight_second):
    frame_count, row_count, col_count, channels = frames_one.shape
    shape_four = (frame_count, row_count, col_count, channels)
    frame_masks = make_masks(clip_ids)
    columns_in = tap_columns(pad_both(frames_one), frame_masks, False, row_count, col_count)
    first_out = jnp.dot(columns_in, weight_first, preferred_element_type=jnp.float32)
    hidden = jax.nn.silu(first_out).astype(jnp.bfloat16).reshape(shape_four)
    columns_hidden = tap_columns(pad_both(hidden), frame_masks, False, row_count, col_count)
    second_out = jnp.dot(columns_hidden, weight_second, preferred_element_type=jnp.float32)
    summed = frames_one.astype(jnp.float32) + second_out.reshape(shape_four)
    pooled = summed.reshape(frame_count, row_count // 2, 2, col_count // 2, 2, channels).mean(axis=(2, 4))
    grad_out = jnp.repeat(jnp.repeat(cot_one, 2, axis=1), 2, axis=2) * jnp.bfloat16(0.25)
    columns_grad = tap_columns(pad_both(grad_out), frame_masks, True, row_count, col_count)
    grad_hidden = jnp.dot(columns_grad, flip_kernel(weight_second), preferred_element_type=jnp.float32)
    sigma = jax.nn.sigmoid(first_out)
    grad_act = (grad_hidden * sigma * (1.0 + first_out * (1.0 - sigma))).astype(jnp.bfloat16)
    columns_back = tap_columns(pad_both(grad_act.reshape(shape_four)), frame_masks, True, row_count, col_count)
    back_term = jnp.dot(columns_back, flip_kernel(weight_first), preferred_element_type=jnp.float32)
    input_grad = grad_out.astype(jnp.float32) + back_term.reshape(shape_four)
    grad_second = jnp.dot(columns_hidden.T, grad_out.reshape(-1, channels), preferred_element_type=jnp.float32)
    grad_first = jnp.dot(columns_in.T, grad_act, preferred_element_type=jnp.float32)
    return (pooled, input_grad, grad_first, grad_second)

def reference(clip_frames, segments, weight_first, weight_second, cotangent):

    def step_group(operands):
        return one_group(operands[0], operands[1], operands[2], weight_first, weight_second)
    pooled, input_grad, firsts, seconds = lax.map(step_group, (clip_frames, segments, cotangent))
    scale = 1.0 / math.sqrt(GROUPS * FRAMES * H * WW)
    grad_first = lax.optimization_barrier(jnp.sum(firsts, axis=0)) * scale
    grad_second = lax.optimization_barrier(jnp.sum(seconds, axis=0)) * scale
    return (pooled, input_grad, grad_first, grad_second)
```

```python
import functools
import math

import jax
import jax.numpy as jnp
from jax import lax
from jax.experimental import pallas as pl
from jax.experimental.pallas import tpu as pltpu
from jax.sharding import PartitionSpec as P

MESH = pl.DeviceIdType.MESH
F32 = jnp.float32
BF16 = jnp.bfloat16


def up16(n):
    return -(-n // 16) * 16


def shifted_cols(cells, step):
    if step == 0:
        return cells
    cols = cells.shape[2]
    col = lax.broadcasted_iota(jnp.int32, cells.shape, 2)
    moved = pltpu.roll(cells, (-step) % cols, 2)
    keep = (col < cols - 1) if step == 1 else (col > 0)
    return jnp.where(keep, moved, 0.0)


def fill_columns(dst, cells, same, reverse):
    rows, frames, cols, ch = cells.shape
    for ci in range(3):
        moved = shifted_cols(cells, (1 - ci) if reverse else (ci - 1))
        for t in range(3):
            zero = jnp.zeros((rows, cols, ch), F32)
            parts = []
            for f in range(frames):
                src = f + t if reverse else f - t
                if src < 0 or src >= frames:
                    parts.append(zero)
                elif t == 0:
                    parts.append(moved[:, src])
                else:
                    parts.append(moved[:, src] * same[t][max(f, src)])
            block = jnp.stack(parts, axis=1).reshape(rows * frames * cols, ch)
            at = (t * 3 + ci) * ch
            dst[:, at : at + ch] = block.astype(BF16)


def conv_dots(cols_ref, w_ref, start, rows, slab, reverse):
    acc = None
    span = w_ref.shape[1] * 3
    for t in range(3):
        for a in range(3):
            at = (start + (2 - a if reverse else a)) * slab
            term = jnp.dot(
                cols_ref[at : at + rows * slab, t * span : (t + 1) * span],
                w_ref[(t * 3 + a) * span : (t * 3 + a + 1) * span, :],
                preferred_element_type=F32,
            )
            acc = term if acc is None else acc + term
    return acc


def kernel(
    cfg,
    seg, x_in, w1, w2, g_in,
    pooled, in_grad, out1, out2,
    x_halo, g_halo, cols_x, cols_h, cols_g, cols_a, w1t, w2t, pool_tmp,
    flat1, flat2, recv_a, sum_a, send_b, recv_b, sum_b, send_c, recv_c, fin,
    h_send, h_recv, a_send, a_recv, b_send, b_recv, c_send, c_recv, d_send, d_recv,
):
    n_tile, n_dp, share, chunk, scale = cfg
    n_z = n_tile // 2
    rows, slab, ch = x_in.shape
    frames = seg.shape[1]
    cols = slab // frames
    tile = lax.axis_index("tile")
    dp = lax.axis_index("dp")
    core = lax.rem(tile, 2)
    z = lax.div(tile, 2)
    flats = (flat1, flat2)
    outs = (out1, out2)

    barrier = pltpu.get_barrier_semaphore()

    def greet(peer):
        pl.semaphore_signal(barrier, inc=1, device_id=peer, device_id_type=MESH)

    @pl.when(tile > 0)
    def _():
        greet({"tile": tile - 1})

    @pl.when(tile < n_tile - 1)
    def _():
        greet({"tile": tile + 1})

    for i in range(1, n_dp):
        greet({"dp": lax.rem(dp + i, n_dp)})
    for j in range(1, n_z):
        greet({"tile": 2 * lax.rem(z + j, n_z) + core})

    span = 3 * ch

    def flip(src, dst):
        for tap in range(27):
            dst[tap * ch : (tap + 1) * ch, :] = src[tap * ch : (tap + 1) * ch, :].T

    flip(w2, w2t)
    for g in range(2):
        sum_a[g, :, share:, :] = jnp.zeros((n_z, sum_a.shape[2] - share, ch), F32)

    @pl.when(tile == 0)
    def _():
        x_halo[0] = jnp.zeros(x_halo.shape[1:], BF16)
        g_halo[0] = jnp.zeros(g_halo.shape[1:], BF16)

    @pl.when(tile == n_tile - 1)
    def _():
        x_halo[1] = jnp.zeros(x_halo.shape[1:], BF16)
        g_halo[1] = jnp.zeros(g_halo.shape[1:], BF16)

    beside = jnp.where(tile > 0, 1, 0) + jnp.where(tile < n_tile - 1, 1, 0)
    pl.semaphore_wait(barrier, n_dp - 1 + n_z - 1 + beside)

    g_rows = g_in.shape[0]

    def halo(side):
        peer = {"tile": tile - 1 if side == 0 else tile + 1}
        return (
            pltpu.make_async_remote_copy(
                src_ref=x_in.at[0:2] if side == 0 else x_in.at[rows - 2 : rows],
                dst_ref=x_halo.at[1 - side],
                send_sem=h_send.at[side], recv_sem=h_recv.at[1 - side],
                device_id=peer, device_id_type=MESH,
            ),
            pltpu.make_async_remote_copy(
                src_ref=g_in.at[0:1] if side == 0 else g_in.at[g_rows - 1 : g_rows],
                dst_ref=g_halo.at[1 - side],
                send_sem=h_send.at[2 + side], recv_sem=h_recv.at[2 + 1 - side],
                device_id=peer, device_id_type=MESH,
            ),
        )

    @pl.when(tile > 0)
    def _():
        for copy in halo(0):
            copy.start()

    @pl.when(tile < n_tile - 1)
    def _():
        for copy in halo(1):
            copy.start()

    flip(w1, w1t)
    same = [None]
    for t in range(1, 3):
        same.append(
            [None] * t
            + [jnp.where(seg[0, f] == seg[0, f - t], 1.0, 0.0).astype(F32) for f in range(t, frames)]
        )

    @pl.when(tile > 0)
    def _():
        for copy in halo(0):
            copy.wait_send()
        for copy in halo(1):
            copy.wait_recv()

    @pl.when(tile < n_tile - 1)
    def _():
        for copy in halo(1):
            copy.wait_send()
        for copy in halo(0):
            copy.wait_recv()

    def four(v):
        return v.reshape(v.shape[0], frames, cols, ch)

    mine = x_in[...].astype(F32)
    x_all = jnp.concatenate([x_halo[0].astype(F32), mine, x_halo[1].astype(F32)], axis=0)
    fill_columns(cols_x, four(x_all), same, False)
    g_all = jnp.concatenate([g_halo[0], g_in[...], g_halo[1]], axis=0).astype(F32)
    g_all = jnp.stack([g_all, g_all], axis=1).reshape(2 * g_all.shape[0], slab, ch)
    fill_columns(cols_g, four(g_all), same, True)

    wide = rows + 2
    first = conv_dots(cols_x, w1, 0, wide, slab, False)
    sigma = 1.0 / (1.0 + jnp.exp(-first))
    top = jnp.where(tile > 0, 1.0, 0.0).astype(F32)
    low = jnp.where(tile < n_tile - 1, 1.0, 0.0).astype(F32)

    def edges(v):
        v = v.reshape(wide, slab, ch)
        return jnp.concatenate([v[:1] * top, v[1:-1], v[-1:] * low], axis=0)

    hidden_grad = conv_dots(cols_g, w2t, 0, wide, slab, True)
    act = edges(hidden_grad * sigma * (1.0 + first * (1.0 - sigma)))
    act_own = act[1 : 1 + rows].reshape(rows * slab, ch).astype(BF16)

    def kernel_grad(flat, cols_ref, start, g):
        for t in range(3):
            for a in range(3):
                at = (start + a) * slab
                flat[(t * 3 + a) * span : (t * 3 + a + 1) * span, :] = lax.dot_general(
                    cols_ref[at : at + rows * slab, t * span : (t + 1) * span],
                    g,
                    (((0,), (0,)), ((), ())),
                    preferred_element_type=F32,
                )

    def copies_a(g):
        return [
            pltpu.make_async_remote_copy(
                src_ref=flats[g].at[pl.ds(pl.multiple_of((2 * k + 1 - core) * share, 8), share)],
                dst_ref=recv_a.at[g, k],
                send_sem=a_send.at[g, k], recv_sem=a_recv.at[g, k],
                device_id={"tile": tile + 1 - 2 * core}, device_id_type=MESH,
            )
            for k in range(n_z)
        ]

    def copies_b(g):
        return [
            pltpu.make_async_remote_copy(
                src_ref=send_b.at[g, i - 1], dst_ref=recv_b.at[g, i - 1],
                send_sem=b_send.at[g, i - 1], recv_sem=b_recv.at[g, i - 1],
                device_id={"dp": lax.rem(dp + i, n_dp)}, device_id_type=MESH,
            )
            for i in range(1, n_dp)
        ]

    def copies_c(g):
        return [
            pltpu.make_async_remote_copy(
                src_ref=send_c.at[g, j - 1], dst_ref=recv_c.at[g, j - 1],
                send_sem=c_send.at[g, j - 1], recv_sem=c_recv.at[g, j - 1],
                device_id={"tile": 2 * lax.rem(z + j, n_z) + core}, device_id_type=MESH,
            )
            for j in range(1, n_z)
        ]

    def part(q):
        return pl.ds(pl.multiple_of(q * chunk, 16), chunk)

    def copies_d(g):
        return [
            pltpu.make_async_remote_copy(
                src_ref=fin.at[g, part(dp)], dst_ref=fin.at[g, part(dp)],
                send_sem=d_send.at[g, i - 1], recv_sem=d_recv.at[g, i - 1],
                device_id={"dp": lax.rem(dp + i, n_dp)}, device_id_type=MESH,
            )
            for i in range(1, n_dp)
        ]

    def start(copies):
        for copy in copies:
            copy.start()

    def wait(copies):
        for copy in copies:
            copy.wait()

    def step_b(g):
        wait(copies_a(g))
        for k in range(n_z):
            own = flats[g][pl.ds(pl.multiple_of((2 * k + core) * share, 8), share), :]
            sum_a[g, k, 0:share, :] = own + recv_a[g, k]
        for i in range(1, n_dp):
            send_b[g, i - 1] = sum_a[g, :, part(lax.rem(dp + i, n_dp)), :].astype(BF16)
        start(copies_b(g))

    def step_c(g):
        wait(copies_b(g))
        total = sum_a[g, :, part(dp), :]
        for i in range(1, n_dp):
            total = total + recv_b[g, i - 1].astype(F32)
        sum_b[g] = total
        for j in range(1, n_z):
            send_c[g, j - 1] = sum_b[g, lax.rem(z + j, n_z)].astype(BF16)
        start(copies_c(g))

    def step_d(g):
        wait(copies_c(g))
        total = sum_b[g, z]
        for j in range(1, n_z):
            total = total + recv_c[g, j - 1].astype(F32)
        fin[g, part(dp), :] = total * scale
        start(copies_d(g))

    kernel_grad(flat1, cols_x, 1, act_own)
    start(copies_a(0))
    hidden = edges(first * sigma)
    fill_columns(cols_h, four(hidden), same, False)
    g_own = g_all[2 : 2 + rows].reshape(rows * slab, ch)
    kernel_grad(flat2, cols_h, 0, g_own.astype(BF16))
    start(copies_a(1))
    step_b(0)
    step_b(1)
    second = conv_dots(cols_h, w2, 0, rows, slab, False)
    summed = mine + second.reshape(rows, slab, ch)
    pairs = rows // 2
    for i in range(pairs):
        pool_tmp[i * slab : (i + 1) * slab, :] = summed[2 * i] + summed[2 * i + 1]
    half = pairs * slab // 2
    pooled[...] = 0.25 * (
        pool_tmp[pl.ds(0, half, stride=2), :] + pool_tmp[pl.ds(1, half, stride=2), :]
    )
    fill_columns(cols_a, four(act), same, True)
    step_c(0)
    back = conv_dots(cols_a, w1t, 0, rows, slab, True)
    in_grad[...] = g_own + back
    step_c(1)
    step_d(0)
    step_d(1)
    for g in range(2):
        wait(copies_d(g))
        outs[g][...] = fin[g, 0:share, :]


def local(n_tile, n_dp, clip_frames, segments, weight_first, weight_second, cotangent):
    _, frames, rows, cols, ch = clip_frames.shape
    slab = frames * cols
    taps = weight_first.shape[0]
    share = taps // n_tile
    chunk = up16(-(-share // n_dp))
    n_z = n_tile // 2
    x = clip_frames[0].transpose(1, 0, 2, 3).reshape(rows, slab, ch)
    g = jnp.repeat(cotangent[0].transpose(1, 0, 2, 3), 2, axis=2) * jnp.bfloat16(0.25)
    g = g.reshape(rows // 2, slab, ch)
    scale = 1.0 / math.sqrt(n_dp * n_tile * rows * slab)
    vmem = pl.BlockSpec(memory_space=pltpu.VMEM)
    cells = rows * slab
    sem = pltpu.SemaphoreType.DMA
    pooled, in_grad, first, second = pl.pallas_call(
        functools.partial(kernel, (n_tile, n_dp, share, chunk, scale)),
        out_shape=(
            jax.ShapeDtypeStruct((cells // 4, ch), F32),
            jax.ShapeDtypeStruct((cells, ch), F32),
            jax.ShapeDtypeStruct((share, ch), F32),
            jax.ShapeDtypeStruct((share, ch), F32),
        ),
        in_specs=[pl.BlockSpec(memory_space=pltpu.SMEM)] + [vmem] * 4,
        out_specs=(vmem,) * 4,
        scratch_shapes=[
            pltpu.VMEM((2, 2, slab, ch), BF16),
            pltpu.VMEM((2, 1, slab, ch), BF16),
            pltpu.VMEM(((rows + 4) * slab, 9 * ch), BF16),
            pltpu.VMEM(((rows + 2) * slab, 9 * ch), BF16),
            pltpu.VMEM(((rows + 4) * slab, 9 * ch), BF16),
            pltpu.VMEM(((rows + 2) * slab, 9 * ch), BF16),
            pltpu.VMEM((taps, ch), BF16),
            pltpu.VMEM((taps, ch), BF16),
            pltpu.VMEM((cells // 2, ch), F32),
            pltpu.VMEM((taps, ch), F32),
            pltpu.VMEM((taps, ch), F32),
            pltpu.VMEM((2, n_z, share, ch), F32),
            pltpu.VMEM((2, n_z, n_dp * chunk, ch), F32),
            pltpu.VMEM((2, n_dp - 1, n_z, chunk, ch), BF16),
            pltpu.VMEM((2, n_dp - 1, n_z, chunk, ch), BF16),
            pltpu.VMEM((2, n_z, chunk, ch), F32),
            pltpu.VMEM((2, n_z - 1, chunk, ch), BF16),
            pltpu.VMEM((2, n_z - 1, chunk, ch), BF16),
            pltpu.VMEM((2, n_dp * chunk, ch), F32),
            sem((4,)), sem((4,)),
            sem((2, n_z)), sem((2, n_z)),
            sem((2, n_dp - 1)), sem((2, n_dp - 1)),
            sem((2, n_z - 1)), sem((2, n_z - 1)),
            sem((2, n_dp - 1)), sem((2, n_dp - 1)),
        ],
        compiler_params=pltpu.CompilerParams(
            collective_id=0, has_side_effects=True, vmem_limit_bytes=50 * 1024 * 1024
        ),
    )(segments, x, weight_first, weight_second, g)
    pooled = pooled.reshape(rows // 2, frames, cols // 2, ch).transpose(1, 0, 2, 3)
    in_grad = in_grad.reshape(rows, frames, cols, ch).transpose(1, 0, 2, 3)
    return (pooled[None], in_grad[None], first, second)


def solution(mesh):
    return jax.shard_map(
        functools.partial(local, mesh.shape["tile"], mesh.shape["dp"]),
        mesh=mesh,
        in_specs=(
            P("dp", None, "tile", None, None),
            P("dp", None),
            P(),
            P(),
            P("dp", None, "tile", None, None),
        ),
        out_specs=(
            P("dp", None, "tile", None, None),
            P("dp", None, "tile", None, None),
            P("tile", None),
            P("tile", None),
        ),
        check_vma=False,
    )
```

```python
import functools
import math

import jax
import jax.numpy as jnp
from jax import lax
from jax.experimental import pallas as pl
from jax.experimental.pallas import tpu as pltpu
from jax.sharding import PartitionSpec as P

MESH = pl.DeviceIdType.MESH
F32 = jnp.float32
BF16 = jnp.bfloat16


def up16(n):
    return -(-n // 16) * 16


def shifted_cols(cells, step):
    if step == 0:
        return cells
    cols = cells.shape[2]
    col = lax.broadcasted_iota(jnp.int32, cells.shape, 2)
    moved = pltpu.roll(cells, (-step) % cols, 2)
    keep = (col < cols - 1) if step == 1 else (col > 0)
    return jnp.where(keep, moved, 0.0)


def fill_columns(dst, cells, same, reverse):
    rows, frames, cols, ch = cells.shape
    for ci in range(3):
        moved = shifted_cols(cells, (1 - ci) if reverse else (ci - 1))
        for t in range(3):
            zero = jnp.zeros((rows, cols, ch), F32)
            parts = []
            for f in range(frames):
                src = f + t if reverse else f - t
                if src < 0 or src >= frames:
                    parts.append(zero)
                elif t == 0:
                    parts.append(moved[:, src])
                else:
                    parts.append(moved[:, src] * same[t][max(f, src)])
            block = jnp.stack(parts, axis=1).reshape(rows * frames * cols, ch)
            at = (t * 3 + ci) * ch
            dst[:, at : at + ch] = block.astype(BF16)


def conv_dots(cols_ref, w_ref, start, rows, slab, reverse):
    acc = None
    span = w_ref.shape[1] * 3
    for t in range(3):
        for a in range(3):
            at = (start + (2 - a if reverse else a)) * slab
            term = jnp.dot(
                cols_ref[at : at + rows * slab, t * span : (t + 1) * span],
                w_ref[(t * 3 + a) * span : (t * 3 + a + 1) * span, :],
                preferred_element_type=F32,
            )
            acc = term if acc is None else acc + term
    return acc


def kernel(
    cfg,
    seg, x_hbm, w1_hbm, w2_hbm, g_in,
    pooled, in_grad, out1, out2,
    x_in, w1, w2, in_sem, x_halo, g_halo, cols_x, cols_h, cols_g, cols_a, w1t, w2t, pool_tmp,
    flat1, flat2, send_a, recv_a, sum_a, send_b, recv_b, sum_b, send_c, recv_c, fin,
    h_send, h_recv, a_send, a_recv, b_send, b_recv, c_send, c_recv, d_send, d_recv,
):
    n_tile, n_dp, share, chunk, scale = cfg
    n_z = n_tile // 2
    rows, frames, cols, ch = x_in.shape
    slab = frames * cols
    tile = lax.axis_index("tile")
    dp = lax.axis_index("dp")
    core = lax.rem(tile, 2)
    z = lax.div(tile, 2)
    flats = (flat1, flat2)
    outs = (out1, out2)

    load_x = [
        pltpu.make_async_copy(x_hbm.at[0, :, r], x_in.at[r], in_sem.at[2 + r]) for r in range(rows)
    ]
    load_w1 = pltpu.make_async_copy(w1_hbm, w1, in_sem.at[0])
    load_w2 = pltpu.make_async_copy(w2_hbm, w2, in_sem.at[1])
    for copy in load_x:
        copy.start()
    load_w1.start()
    load_w2.start()

    barrier = pltpu.get_barrier_semaphore()

    def greet(peer):
        pl.semaphore_signal(barrier, inc=1, device_id=peer, device_id_type=MESH)

    @pl.when(tile > 0)
    def _():
        greet({"tile": tile - 1})

    @pl.when(tile < n_tile - 1)
    def _():
        greet({"tile": tile + 1})

    for i in range(1, n_dp):
        greet({"dp": lax.rem(dp + i, n_dp)})
    for j in range(1, n_z):
        greet({"tile": 2 * lax.rem(z + j, n_z) + core})

    span = 3 * ch

    def flip(src, dst):
        for tap in range(27):
            dst[tap * ch : (tap + 1) * ch, :] = src[tap * ch : (tap + 1) * ch, :].T

    for g in range(2):
        if sum_a.shape[2] > share:
            sum_a[g, :, share:, :] = jnp.zeros((n_z, sum_a.shape[2] - share, ch), F32)
        if send_a.shape[2] > share:
            send_a[g, :, share:, :] = jnp.zeros((n_z, send_a.shape[2] - share, ch), BF16)

    @pl.when(tile == 0)
    def _():
        x_halo[0] = jnp.zeros(x_halo.shape[1:], BF16)
        g_halo[0] = jnp.zeros(g_halo.shape[1:], BF16)

    @pl.when(tile == n_tile - 1)
    def _():
        x_halo[1] = jnp.zeros(x_halo.shape[1:], BF16)
        g_halo[1] = jnp.zeros(g_halo.shape[1:], BF16)

    for copy in load_x:
        copy.wait()
    beside = jnp.where(tile > 0, 1, 0) + jnp.where(tile < n_tile - 1, 1, 0)
    pl.semaphore_wait(barrier, n_dp - 1 + n_z - 1 + beside)

    g_rows = g_in.shape[0]

    def halo(side):
        peer = {"tile": tile - 1 if side == 0 else tile + 1}
        return (
            pltpu.make_async_remote_copy(
                src_ref=x_in.at[0:2] if side == 0 else x_in.at[rows - 2 : rows],
                dst_ref=x_halo.at[1 - side],
                send_sem=h_send.at[side], recv_sem=h_recv.at[1 - side],
                device_id=peer, device_id_type=MESH,
            ),
            pltpu.make_async_remote_copy(
                src_ref=g_in.at[0:1] if side == 0 else g_in.at[g_rows - 1 : g_rows],
                dst_ref=g_halo.at[1 - side],
                send_sem=h_send.at[2 + side], recv_sem=h_recv.at[2 + 1 - side],
                device_id=peer, device_id_type=MESH,
            ),
        )

    @pl.when(tile > 0)
    def _():
        for copy in halo(0):
            copy.start()

    @pl.when(tile < n_tile - 1)
    def _():
        for copy in halo(1):
            copy.start()

    load_w1.wait()
    load_w2.wait()
    flip(w2, w2t)
    flip(w1, w1t)
    same = [None]
    for t in range(1, 3):
        same.append(
            [None] * t
            + [jnp.where(seg[0, f] == seg[0, f - t], 1.0, 0.0).astype(F32) for f in range(t, frames)]
        )

    @pl.when(tile > 0)
    def _():
        for copy in halo(0):
            copy.wait_send()
        for copy in halo(1):
            copy.wait_recv()

    @pl.when(tile < n_tile - 1)
    def _():
        for copy in halo(1):
            copy.wait_send()
        for copy in halo(0):
            copy.wait_recv()

    def four(v):
        return v.reshape(v.shape[0], frames, cols, ch)

    mine = x_in[...].astype(F32)
    x_all = jnp.concatenate([x_halo[0].astype(F32), mine, x_halo[1].astype(F32)], axis=0)
    fill_columns(cols_x, x_all, same, False)
    g_all = jnp.concatenate([g_halo[0], g_in[...], g_halo[1]], axis=0).astype(F32)
    g_all = jnp.stack([g_all, g_all], axis=1).reshape(2 * g_all.shape[0], slab, ch)

    wide = rows + 2
    first = conv_dots(cols_x, w1, 0, wide, slab, False)
    sigma = 1.0 / (1.0 + jnp.exp(-first))
    top = jnp.where(tile > 0, 1.0, 0.0).astype(F32)
    low = jnp.where(tile < n_tile - 1, 1.0, 0.0).astype(F32)

    def edges(v):
        v = v.reshape(wide, slab, ch)
        return jnp.concatenate([v[:1] * top, v[1:-1], v[-1:] * low], axis=0)

    def kernel_grad(flat, cols_ref, start, g):
        for t in range(3):
            for a in range(3):
                at = (start + a) * slab
                flat[(t * 3 + a) * span : (t * 3 + a + 1) * span, :] = lax.dot_general(
                    cols_ref[at : at + rows * slab, t * span : (t + 1) * span],
                    g,
                    (((0,), (0,)), ((), ())),
                    preferred_element_type=F32,
                )

    def copies_a(g):
        return [
            pltpu.make_async_remote_copy(
                src_ref=send_a.at[g, k],
                dst_ref=recv_a.at[g, k],
                send_sem=a_send.at[g, k], recv_sem=a_recv.at[g, k],
                device_id={"tile": tile + 1 - 2 * core}, device_id_type=MESH,
            )
            for k in range(n_z)
        ]

    def copies_b(g):
        return [
            pltpu.make_async_remote_copy(
                src_ref=send_b.at[g, i - 1], dst_ref=recv_b.at[g, i - 1],
                send_sem=b_send.at[g, i - 1], recv_sem=b_recv.at[g, i - 1],
                device_id={"dp": lax.rem(dp + i, n_dp)}, device_id_type=MESH,
            )
            for i in range(1, n_dp)
        ]

    def copies_c(g):
        return [
            pltpu.make_async_remote_copy(
                src_ref=send_c.at[g, j - 1], dst_ref=recv_c.at[g, j - 1],
                send_sem=c_send.at[g, j - 1], recv_sem=c_recv.at[g, j - 1],
                device_id={"tile": 2 * lax.rem(z + j, n_z) + core}, device_id_type=MESH,
            )
            for j in range(1, n_z)
        ]

    def part(q):
        return pl.ds(pl.multiple_of(q * chunk, 16), chunk)

    def copies_d(g):
        return [
            pltpu.make_async_remote_copy(
                src_ref=fin.at[g, part(dp)], dst_ref=fin.at[g, part(dp)],
                send_sem=d_send.at[g, i - 1], recv_sem=d_recv.at[g, i - 1],
                device_id={"dp": lax.rem(dp + i, n_dp)}, device_id_type=MESH,
            )
            for i in range(1, n_dp)
        ]

    def start(copies):
        for copy in copies:
            copy.start()

    def wait(copies):
        for copy in copies:
            copy.wait()

    def step_b(g):
        wait(copies_a(g))
        for k in range(n_z):
            own = flats[g][pl.ds(pl.multiple_of((2 * k + core) * share, 8), share), :]
            sum_a[g, k, 0:share, :] = own + recv_a[g, k, 0:share].astype(F32)
        for i in range(1, n_dp):
            send_b[g, i - 1] = sum_a[g, :, part(lax.rem(dp + i, n_dp)), :].astype(BF16)
        start(copies_b(g))

    def step_c(g):
        wait(copies_b(g))
        total = sum_a[g, :, part(dp), :]
        for i in range(1, n_dp):
            total = total + recv_b[g, i - 1].astype(F32)
        sum_b[g] = total
        for j in range(1, n_z):
            send_c[g, j - 1] = sum_b[g, lax.rem(z + j, n_z)].astype(BF16)
        start(copies_c(g))

    def step_d(g):
        wait(copies_c(g))
        total = sum_b[g, z]
        for j in range(1, n_z):
            total = total + recv_c[g, j - 1].astype(F32)
        fin[g, part(dp), :] = total * scale
        start(copies_d(g))

    def step_a(g):
        for k, copy in enumerate(copies_a(g)):
            at = pl.ds(pl.multiple_of((2 * k + 1 - core) * share, 8), share)
            send_a[g, k, 0:share, :] = flats[g][at, :].astype(BF16)
            copy.start()

    hidden = edges(first * sigma)
    fill_columns(cols_h, four(hidden), same, False)
    g_own = g_all[2 : 2 + rows].reshape(rows * slab, ch)
    kernel_grad(flat2, cols_h, 0, g_own.astype(BF16))
    step_a(1)
    fill_columns(cols_g, four(g_all), same, True)
    hidden_grad = conv_dots(cols_g, w2t, 0, wide, slab, True)
    act = edges(hidden_grad * sigma * (1.0 + first * (1.0 - sigma)))
    act_own = act[1 : 1 + rows].reshape(rows * slab, ch).astype(BF16)

    step_b(1)
    kernel_grad(flat1, cols_x, 1, act_own)
    step_a(0)
    fill_columns(cols_a, four(act), same, True)
    step_b(0)
    second = conv_dots(cols_h, w2, 0, rows, slab, False)
    summed = mine.reshape(rows, slab, ch) + second.reshape(rows, slab, ch)
    pairs = rows // 2
    for i in range(pairs):
        pool_tmp[i * slab : (i + 1) * slab, :] = summed[2 * i] + summed[2 * i + 1]
    for i in range(pairs):
        for f in range(frames):
            at = i * slab + f * cols
            pooled[0, f, i] = 0.25 * (
                pool_tmp[pl.ds(at, cols // 2, stride=2), :]
                + pool_tmp[pl.ds(at + 1, cols // 2, stride=2), :]
            )
    step_c(1)
    back = conv_dots(cols_a, w1t, 0, rows, slab, True)
    total = (g_own + back).reshape(rows, frames, cols, ch)
    for r in range(rows):
        in_grad[0, :, r] = total[r]
    step_c(0)
    step_d(1)
    step_d(0)
    for g in (1, 0):
        wait(copies_d(g))
        outs[g][...] = fin[g, 0:share, :]


def hand_on(*refs):
    count = len(refs) // 2
    sems = refs[-1]
    copies = [pltpu.make_async_copy(refs[i], refs[count + i], sems.at[i]) for i in range(count)]
    for copy in copies:
        copy.start()
    for copy in copies:
        copy.wait()


def local(n_tile, n_dp, clip_frames, segments, weight_first, weight_second, cotangent):
    _, frames, rows, cols, ch = clip_frames.shape
    slab = frames * cols
    taps = weight_first.shape[0]
    share = taps // n_tile
    chunk = up16(-(-share // n_dp))
    n_z = n_tile // 2
    g = jnp.repeat(cotangent[0].transpose(1, 0, 2, 3), 2, axis=2) * jnp.bfloat16(0.25)
    g = g.reshape(rows // 2, slab, ch)
    scale = 1.0 / math.sqrt(n_dp * n_tile * rows * slab)
    vmem = pl.BlockSpec(memory_space=pltpu.VMEM)
    cells = rows * slab
    sem = pltpu.SemaphoreType.DMA
    anywhere = pl.BlockSpec(memory_space=pl.ANY)
    shapes = (
        jax.ShapeDtypeStruct((1, frames, rows // 2, cols // 2, ch), F32),
        jax.ShapeDtypeStruct((1, frames, rows, cols, ch), F32),
        jax.ShapeDtypeStruct((share, ch), F32),
        jax.ShapeDtypeStruct((share, ch), F32),
    )
    results = pl.pallas_call(
        functools.partial(kernel, (n_tile, n_dp, share, chunk, scale)),
        out_shape=shapes,
        in_specs=[pl.BlockSpec(memory_space=pltpu.SMEM)] + [anywhere] * 3 + [vmem],
        out_specs=(vmem,) * 4,
        scratch_shapes=[
            pltpu.VMEM((rows, frames, cols, ch), BF16),
            pltpu.VMEM((taps, ch), BF16),
            pltpu.VMEM((taps, ch), BF16),
            sem((2 + rows,)),
            pltpu.VMEM((2, 2, frames, cols, ch), BF16),
            pltpu.VMEM((2, 1, slab, ch), BF16),
            pltpu.VMEM(((rows + 4) * slab, 9 * ch), BF16),
            pltpu.VMEM(((rows + 2) * slab, 9 * ch), BF16),
            pltpu.VMEM(((rows + 4) * slab, 9 * ch), BF16),
            pltpu.VMEM(((rows + 2) * slab, 9 * ch), BF16),
            pltpu.VMEM((taps, ch), BF16),
            pltpu.VMEM((taps, ch), BF16),
            pltpu.VMEM((cells // 2, ch), F32),
            pltpu.VMEM((taps, ch), F32),
            pltpu.VMEM((taps, ch), F32),
            pltpu.VMEM((2, n_z, up16(share), ch), BF16),
            pltpu.VMEM((2, n_z, up16(share), ch), BF16),
            pltpu.VMEM((2, n_z, n_dp * chunk, ch), F32),
            pltpu.VMEM((2, n_dp - 1, n_z, chunk, ch), BF16),
            pltpu.VMEM((2, n_dp - 1, n_z, chunk, ch), BF16),
            pltpu.VMEM((2, n_z, chunk, ch), F32),
            pltpu.VMEM((2, n_z - 1, chunk, ch), BF16),
            pltpu.VMEM((2, n_z - 1, chunk, ch), BF16),
            pltpu.VMEM((2, n_dp * chunk, ch), F32),
            sem((4,)), sem((4,)),
            sem((2, n_z)), sem((2, n_z)),
            sem((2, n_dp - 1)), sem((2, n_dp - 1)),
            sem((2, n_z - 1)), sem((2, n_z - 1)),
            sem((2, n_dp - 1)), sem((2, n_dp - 1)),
        ],
        compiler_params=pltpu.CompilerParams(
            collective_id=0, has_side_effects=True, vmem_limit_bytes=50 * 1024 * 1024
        ),
    )(segments, clip_frames, weight_first, weight_second, g)
    return pl.pallas_call(
        hand_on,
        out_shape=shapes,
        in_specs=[anywhere] * 4,
        out_specs=(anywhere,) * 4,
        scratch_shapes=[sem((4,))],
    )(*results)


def solution(mesh):
    return jax.shard_map(
        functools.partial(local, mesh.shape["tile"], mesh.shape["dp"]),
        mesh=mesh,
        in_specs=(
            P("dp", None, "tile", None, None),
            P("dp", None),
            P(),
            P(),
            P("dp", None, "tile", None, None),
        ),
        out_specs=(
            P("dp", None, "tile", None, None),
            P("dp", None, "tile", None, None),
            P("tile", None),
            P("tile", None),
        ),
        check_vma=False,
    )
```

```python
import functools
import math

import jax
import jax.numpy as jnp
from jax import lax
from jax.experimental import pallas as pl
from jax.experimental.pallas import tpu as pltpu
from jax.sharding import PartitionSpec as P

MESH = pl.DeviceIdType.MESH
F32 = jnp.float32
BF16 = jnp.bfloat16


def up16(n):
    return -(-n // 16) * 16


def shifted_cols(cells, step):
    if step == 0:
        return cells
    cols = cells.shape[2]
    col = lax.broadcasted_iota(jnp.int32, cells.shape, 2)
    moved = pltpu.roll(cells, (-step) % cols, 2)
    keep = (col < cols - 1) if step == 1 else (col > 0)
    return jnp.where(keep, moved, 0.0)


def fill_columns(dst, cells, same, reverse):
    rows, frames, cols, ch = cells.shape
    for ci in range(3):
        moved = shifted_cols(cells, (1 - ci) if reverse else (ci - 1))
        for t in range(3):
            zero = jnp.zeros((rows, cols, ch), F32)
            parts = []
            for f in range(frames):
                src = f + t if reverse else f - t
                if src < 0 or src >= frames:
                    parts.append(zero)
                elif t == 0:
                    parts.append(moved[:, src])
                else:
                    parts.append(moved[:, src] * same[t][max(f, src)])
            block = jnp.stack(parts, axis=1).reshape(rows * frames * cols, ch)
            at = (t * 3 + ci) * ch
            dst[:, at : at + ch] = block.astype(BF16)


def conv_dots(cols_ref, w_ref, start, rows, slab, reverse):
    acc = None
    span = w_ref.shape[1] * 3
    for t in range(3):
        for a in range(3):
            at = (start + (2 - a if reverse else a)) * slab
            term = jnp.dot(
                cols_ref[at : at + rows * slab, t * span : (t + 1) * span],
                w_ref[(t * 3 + a) * span : (t * 3 + a + 1) * span, :],
                preferred_element_type=F32,
            )
            acc = term if acc is None else acc + term
    return acc


def kernel(
    cfg,
    seg, x_hbm, w1_hbm, w2_hbm, g_in,
    pooled, in_grad, out1, out2,
    x_in, w1, w2, in_sem, x_halo, g_halo, cols_x, cols_h, cols_g, cols_a, w1t, w2t, pool_tmp,
    flat1, flat2, send_a, recv_a, sum_a, send_b, recv_b, sum_b, send_c, recv_c, fin,
    h_send, h_recv, a_send, a_recv, b_send, b_recv, c_send, c_recv, d_send, d_recv,
):
    n_tile, n_dp, share, chunk, scale = cfg
    n_z = n_tile // 2
    rows, frames, cols, ch = x_in.shape
    slab = frames * cols
    tile = lax.axis_index("tile")
    dp = lax.axis_index("dp")
    core = lax.rem(tile, 2)
    z = lax.div(tile, 2)
    flats = (flat1, flat2)
    outs = (out1, out2)

    load_x = [
        pltpu.make_async_copy(x_hbm.at[0, :, r], x_in.at[r], in_sem.at[2 + r]) for r in range(rows)
    ]
    load_w1 = pltpu.make_async_copy(w1_hbm, w1, in_sem.at[0])
    load_w2 = pltpu.make_async_copy(w2_hbm, w2, in_sem.at[1])
    for copy in load_x:
        copy.start()
    load_w1.start()
    load_w2.start()

    barrier = pltpu.get_barrier_semaphore()

    def greet(peer):
        pl.semaphore_signal(barrier, inc=1, device_id=peer, device_id_type=MESH)

    @pl.when(tile > 0)
    def _():
        greet({"tile": tile - 1})

    @pl.when(tile < n_tile - 1)
    def _():
        greet({"tile": tile + 1})

    for i in range(1, n_dp):
        greet({"dp": lax.rem(dp + i, n_dp)})
    for j in range(1, n_z):
        greet({"tile": 2 * lax.rem(z + j, n_z) + core})

    span = 3 * ch

    def flip(src, dst):
        for tap in range(27):
            dst[tap * ch : (tap + 1) * ch, :] = src[tap * ch : (tap + 1) * ch, :].T

    for g in range(2):
        if sum_a.shape[2] > share:
            sum_a[g, :, share:, :] = jnp.zeros((n_z, sum_a.shape[2] - share, ch), F32)
        if send_a.shape[2] > share:
            send_a[g, :, share:, :] = jnp.zeros((n_z, send_a.shape[2] - share, ch), BF16)

    @pl.when(tile == 0)
    def _():
        x_halo[0] = jnp.zeros(x_halo.shape[1:], BF16)
        g_halo[0] = jnp.zeros(g_halo.shape[1:], BF16)

    @pl.when(tile == n_tile - 1)
    def _():
        x_halo[1] = jnp.zeros(x_halo.shape[1:], BF16)
        g_halo[1] = jnp.zeros(g_halo.shape[1:], BF16)

    for copy in load_x:
        copy.wait()
    beside = jnp.where(tile > 0, 1, 0) + jnp.where(tile < n_tile - 1, 1, 0)
    pl.semaphore_wait(barrier, n_dp - 1 + n_z - 1 + beside)

    g_rows = g_in.shape[0]

    def halo(side):
        peer = {"tile": tile - 1 if side == 0 else tile + 1}
        return (
            pltpu.make_async_remote_copy(
                src_ref=x_in.at[0:2] if side == 0 else x_in.at[rows - 2 : rows],
                dst_ref=x_halo.at[1 - side],
                send_sem=h_send.at[side], recv_sem=h_recv.at[1 - side],
                device_id=peer, device_id_type=MESH,
            ),
            pltpu.make_async_remote_copy(
                src_ref=g_in.at[0:1] if side == 0 else g_in.at[g_rows - 1 : g_rows],
                dst_ref=g_halo.at[1 - side],
                send_sem=h_send.at[2 + side], recv_sem=h_recv.at[2 + 1 - side],
                device_id=peer, device_id_type=MESH,
            ),
        )

    @pl.when(tile > 0)
    def _():
        for copy in halo(0):
            copy.start()

    @pl.when(tile < n_tile - 1)
    def _():
        for copy in halo(1):
            copy.start()

    load_w1.wait()
    load_w2.wait()
    flip(w2, w2t)
    flip(w1, w1t)
    same = [None]
    for t in range(1, 3):
        same.append(
            [None] * t
            + [jnp.where(seg[0, f] == seg[0, f - t], 1.0, 0.0).astype(F32) for f in range(t, frames)]
        )

    @pl.when(tile > 0)
    def _():
        for copy in halo(0):
            copy.wait_send()
        for copy in halo(1):
            copy.wait_recv()

    @pl.when(tile < n_tile - 1)
    def _():
        for copy in halo(1):
            copy.wait_send()
        for copy in halo(0):
            copy.wait_recv()

    def four(v):
        return v.reshape(v.shape[0], frames, cols, ch)

    mine = x_in[...].astype(F32)
    x_all = jnp.concatenate([x_halo[0].astype(F32), mine, x_halo[1].astype(F32)], axis=0)
    fill_columns(cols_x, x_all, same, False)
    g_all = jnp.concatenate([g_halo[0], g_in[...], g_halo[1]], axis=0).astype(F32)
    g_all = jnp.stack([g_all, g_all], axis=1).reshape(2 * g_all.shape[0], slab, ch)

    wide = rows + 2
    first = conv_dots(cols_x, w1, 0, wide, slab, False)
    sigma = 1.0 / (1.0 + jnp.exp(-first))
    top = jnp.where(tile > 0, 1.0, 0.0).astype(F32)
    low = jnp.where(tile < n_tile - 1, 1.0, 0.0).astype(F32)

    def edges(v):
        v = v.reshape(wide, slab, ch)
        return jnp.concatenate([v[:1] * top, v[1:-1], v[-1:] * low], axis=0)

    def kernel_grad(flat, cols_ref, start, g):
        for t in range(3):
            for a in range(3):
                at = (start + a) * slab
                flat[(t * 3 + a) * span : (t * 3 + a + 1) * span, :] = lax.dot_general(
                    cols_ref[at : at + rows * slab, t * span : (t + 1) * span],
                    g,
                    (((0,), (0,)), ((), ())),
                    preferred_element_type=F32,
                )

    def copies_a(g):
        return [
            pltpu.make_async_remote_copy(
                src_ref=send_a.at[g, k],
                dst_ref=recv_a.at[g, k],
                send_sem=a_send.at[g, k], recv_sem=a_recv.at[g, k],
                device_id={"tile": tile + 1 - 2 * core}, device_id_type=MESH,
            )
            for k in range(n_z)
        ]

    def copies_b(g):
        return [
            pltpu.make_async_remote_copy(
                src_ref=send_b.at[g, i - 1], dst_ref=recv_b.at[g, i - 1],
                send_sem=b_send.at[g, i - 1], recv_sem=b_recv.at[g, i - 1],
                device_id={"dp": lax.rem(dp + i, n_dp)}, device_id_type=MESH,
            )
            for i in range(1, n_dp)
        ]

    def copies_c(g):
        return [
            pltpu.make_async_remote_copy(
                src_ref=send_c.at[g, j - 1], dst_ref=recv_c.at[g, j - 1],
                send_sem=c_send.at[g, j - 1], recv_sem=c_recv.at[g, j - 1],
                device_id={"tile": 2 * lax.rem(z + j, n_z) + core}, device_id_type=MESH,
            )
            for j in range(1, n_z)
        ]

    def part(q):
        return pl.ds(pl.multiple_of(q * chunk, 16), chunk)

    def copies_d(g):
        return [
            pltpu.make_async_remote_copy(
                src_ref=fin.at[g, part(dp)], dst_ref=fin.at[g, part(dp)],
                send_sem=d_send.at[g, i - 1], recv_sem=d_recv.at[g, i - 1],
                device_id={"dp": lax.rem(dp + i, n_dp)}, device_id_type=MESH,
            )
            for i in range(1, n_dp)
        ]

    def start(copies):
        for copy in copies:
            copy.start()

    def wait(copies):
        for copy in copies:
            copy.wait()

    def step_b(g):
        wait(copies_a(g))
        for k in range(n_z):
            own = flats[g][pl.ds(pl.multiple_of((2 * k + core) * share, 8), share), :]
            sum_a[g, k, 0:share, :] = own + recv_a[g, k, 0:share].astype(F32)
        for i in range(1, n_dp):
            send_b[g, i - 1] = sum_a[g, :, part(lax.rem(dp + i, n_dp)), :].astype(BF16)
        start(copies_b(g))

    def step_c(g):
        wait(copies_b(g))
        total = sum_a[g, :, part(dp), :]
        for i in range(1, n_dp):
            total = total + recv_b[g, i - 1].astype(F32)
        sum_b[g] = total
        for j in range(1, n_z):
            send_c[g, j - 1] = sum_b[g, lax.rem(z + j, n_z)].astype(BF16)
        start(copies_c(g))

    def step_d(g):
        wait(copies_c(g))
        total = sum_b[g, z]
        for j in range(1, n_z):
            total = total + recv_c[g, j - 1].astype(F32)
        fin[g, part(dp), :] = total * scale
        start(copies_d(g))

    def step_a(g):
        for k, copy in enumerate(copies_a(g)):
            at = pl.ds(pl.multiple_of((2 * k + 1 - core) * share, 8), share)
            send_a[g, k, 0:share, :] = flats[g][at, :].astype(BF16)
            copy.start()

    hidden = edges(first * sigma)
    fill_columns(cols_h, four(hidden), same, False)
    g_own = g_all[2 : 2 + rows].reshape(rows * slab, ch)
    kernel_grad(flat2, cols_h, 0, g_own.astype(BF16))
    step_a(1)
    fill_columns(cols_g, four(g_all), same, True)
    hidden_grad = conv_dots(cols_g, w2t, 0, wide, slab, True)
    act = edges(hidden_grad * sigma * (1.0 + first * (1.0 - sigma)))
    act_own = act[1 : 1 + rows].reshape(rows * slab, ch).astype(BF16)

    step_b(1)
    kernel_grad(flat1, cols_x, 1, act_own)
    step_a(0)
    fill_columns(cols_a, four(act), same, True)
    step_b(0)
    second = conv_dots(cols_h, w2, 0, rows, slab, False)
    summed = mine.reshape(rows, slab, ch) + second.reshape(rows, slab, ch)
    pairs = rows // 2
    for i in range(pairs):
        pool_tmp[i * slab : (i + 1) * slab, :] = summed[2 * i] + summed[2 * i + 1]
    for i in range(pairs):
        for f in range(frames):
            at = i * slab + f * cols
            pooled[0, f, i] = 0.25 * (
                pool_tmp[pl.ds(at, cols // 2, stride=2), :]
                + pool_tmp[pl.ds(at + 1, cols // 2, stride=2), :]
            )
    step_c(1)
    back = conv_dots(cols_a, w1t, 0, rows, slab, True)
    total = (g_own + back).reshape(rows, frames, cols, ch)
    for r in range(rows):
        in_grad[0, :, r] = total[r]
    step_c(0)
    step_d(1)
    step_d(0)
    for g in (1, 0):
        wait(copies_d(g))
        outs[g][...] = fin[g, 0:share, :]


def local(n_tile, n_dp, clip_frames, segments, weight_first, weight_second, cotangent):
    _, frames, rows, cols, ch = clip_frames.shape
    slab = frames * cols
    taps = weight_first.shape[0]
    share = taps // n_tile
    chunk = up16(-(-share // n_dp))
    n_z = n_tile // 2
    g = jnp.repeat(cotangent[0].transpose(1, 0, 2, 3), 2, axis=2) * jnp.bfloat16(0.25)
    g = g.reshape(rows // 2, slab, ch)
    scale = 1.0 / math.sqrt(n_dp * n_tile * rows * slab)
    vmem = pl.BlockSpec(memory_space=pltpu.VMEM)
    cells = rows * slab
    sem = pltpu.SemaphoreType.DMA
    anywhere = pl.BlockSpec(memory_space=pltpu.HBM)
    shapes = (
        jax.ShapeDtypeStruct((1, frames, rows // 2, cols // 2, ch), F32),
        jax.ShapeDtypeStruct((1, frames, rows, cols, ch), F32),
        jax.ShapeDtypeStruct((share, ch), F32),
        jax.ShapeDtypeStruct((share, ch), F32),
    )
    results = pl.pallas_call(
        functools.partial(kernel, (n_tile, n_dp, share, chunk, scale)),
        out_shape=shapes,
        in_specs=[pl.BlockSpec(memory_space=pltpu.SMEM)] + [anywhere] * 3 + [vmem],
        out_specs=(vmem,) * 4,
        scratch_shapes=[
            pltpu.VMEM((rows, frames, cols, ch), BF16),
            pltpu.VMEM((taps, ch), BF16),
            pltpu.VMEM((taps, ch), BF16),
            sem((2 + rows,)),
            pltpu.VMEM((2, 2, frames, cols, ch), BF16),
            pltpu.VMEM((2, 1, slab, ch), BF16),
            pltpu.VMEM(((rows + 4) * slab, 9 * ch), BF16),
            pltpu.VMEM(((rows + 2) * slab, 9 * ch), BF16),
            pltpu.VMEM(((rows + 4) * slab, 9 * ch), BF16),
            pltpu.VMEM(((rows + 2) * slab, 9 * ch), BF16),
            pltpu.VMEM((taps, ch), BF16),
            pltpu.VMEM((taps, ch), BF16),
            pltpu.VMEM((cells // 2, ch), F32),
            pltpu.VMEM((taps, ch), F32),
            pltpu.VMEM((taps, ch), F32),
            pltpu.VMEM((2, n_z, up16(share), ch), BF16),
            pltpu.VMEM((2, n_z, up16(share), ch), BF16),
            pltpu.VMEM((2, n_z, n_dp * chunk, ch), F32),
            pltpu.VMEM((2, n_dp - 1, n_z, chunk, ch), BF16),
            pltpu.VMEM((2, n_dp - 1, n_z, chunk, ch), BF16),
            pltpu.VMEM((2, n_z, chunk, ch), F32),
            pltpu.VMEM((2, n_z - 1, chunk, ch), BF16),
            pltpu.VMEM((2, n_z - 1, chunk, ch), BF16),
            pltpu.VMEM((2, n_dp * chunk, ch), F32),
            sem((4,)), sem((4,)),
            sem((2, n_z)), sem((2, n_z)),
            sem((2, n_dp - 1)), sem((2, n_dp - 1)),
            sem((2, n_z - 1)), sem((2, n_z - 1)),
            sem((2, n_dp - 1)), sem((2, n_dp - 1)),
        ],
        compiler_params=pltpu.CompilerParams(
            collective_id=0, has_side_effects=True, vmem_limit_bytes=50 * 1024 * 1024
        ),
    )(segments, clip_frames, weight_first, weight_second, g)
    return tuple(results)


def solution(mesh):
    return jax.shard_map(
        functools.partial(local, mesh.shape["tile"], mesh.shape["dp"]),
        mesh=mesh,
        in_specs=(
            P("dp", None, "tile", None, None),
            P("dp", None),
            P(),
            P(),
            P("dp", None, "tile", None, None),
        ),
        out_specs=(
            P("dp", None, "tile", None, None),
            P("dp", None, "tile", None, None),
            P("tile", None),
            P("tile", None),
        ),
        check_vma=False,
    )
```
